512 devices in a mesh: ctx: 256 (over y_hi, z, x, core), head: 2 (over y_lo).
Axes of the slice: x: 4, y: 4 (y_hi: 2, y_lo: 2; y = y_hi * 2 + y_lo), z: 16, core: 2. Of those that a mesh axis runs over, the one named last changes fastest.
Arguments:
- queries: bfloat16 [65536, 4096], P('ctx', 'head')
- keys: bfloat16 [65536, 1024], P(('ctx', 'head'))
- values: bfloat16 [65536, 1024], P(('ctx', 'head')), may hold values from -6 to 6
- segments: int32 [65536], replicated, may hold values from 0 to 127, never falling along the last dimension, each value on 1 to 1024 neighbouring positions
Outputs:
- attended: bfloat16 [65536, 4096], P('ctx', 'head')
The draws below stay inside these ranges and needn't reach their ends.
Inputs may be any that keep to these rules, and one draw needn't show every extreme that they name: `segments`: ids never fall along the sequence; each document holds 1 to 1024 tokens and one holds exactly 1024.
All inputs are finite; a program needn't handle non-finite values.
Results may differ from the reference program's by a relative error of at most 0.0045.
Values may be sent and summed in bfloat16 or wider, within the bound.
No kernel may reach another device: no remote copies, remote signals or barrier semaphores. Data moves between devices by JAX's collectives and lax.ppermute only.
A program may use at most 64 MiB of HBM per device.

```python
import math
import jax
import jax.numpy as jnp
import numpy as np
from jax import lax

H = 32
KVH = 8
HD = 128
BLOCK = 256
TOKENS = 65536
DOCS = 128
MOST_DOC = 1024


def base_keys(key):
    return jnp.clip(jax.random.normal(key, (TOKENS, KVH * HD), jnp.float32), -6.0, 6.0)


def draw_keys(key, part):
    drawn = base_keys(key)
    result = drawn
    return result.astype(jnp.bfloat16)


def draw_queries(key, part):
    key = jax.random.fold_in(key, 3)
    result = jnp.clip(jax.random.normal(key, (TOKENS, H * HD), jnp.float32), -6.0, 6.0)
    return result.astype(jnp.bfloat16)


def block_scale(stream_key, dims, shards, smallest, top_value):
    loudness, own = 1.0, jax.random.fold_in(stream_key, 6)
    for axis_at, blocks in shards:
        steps = jnp.exp(jax.random.uniform(jax.random.fold_in(own, axis_at), (blocks,), jnp.float32, smallest / len(shards), top_value / len(shards)))
        loudness = loudness * jnp.repeat(steps, dims[axis_at] // blocks).reshape([-1 if axis == axis_at else 1 for axis in range(len(dims))])
    return loudness


def profile(number_of, total, reach, lean):
    weights = [(1 << 20) // math.isqrt(rank ** lean) + 1 for rank in range(2, number_of + 1)]
    rest, counts = total - reach - (number_of - 1), [1] * (number_of - 1)
    while rest > 0:
        free = [i for i in range(number_of - 1) if counts[i] < reach]
        whole, remaining = sum([weights[i] for i in free]), rest
        for i in free:
            more = min(reach - counts[i], max(1, remaining * weights[i] // whole), rest)
            counts[i] = counts[i] + more
            rest = rest - more
    return np.array([reach] + counts)


def ragged_sizes(own_key, number_of, total, limit, skew):
    if number_of == 2:
        one = jax.random.randint(own_key, (), max(1, total - limit), min(limit, total - 1) + 1)
        return jnp.stack([one, total - one])
    sizes = jnp.asarray(profile(number_of, total, limit, skew), jnp.int32)
    pairs = (number_of - 1) // 2
    giver, receiver = sizes[1:1 + 2 * pairs:2], sizes[2:2 + 2 * pairs:2]
    room = jnp.minimum(giver - 1, limit - receiver)
    passed = jax.random.randint(jax.random.fold_in(own_key, 1), (pairs,), 0, 1 << 20) % (room + 1)
    sizes = sizes.at[1:1 + 2 * pairs:2].set(giver - passed).at[2:2 + 2 * pairs:2].set(receiver + passed)
    return sizes[jax.random.permutation(jax.random.fold_in(own_key, 2), number_of)]


def gaussian(rng, extent, scale, most, pieces=(), held_as=jnp.bfloat16):
    values = scale * jax.random.normal(rng, extent, jnp.float32)
    if pieces:
        values = values * block_scale(rng, extent, pieces, -0.22, 0.18)
    return jnp.clip(values, -most, most).astype(held_as)


def setup_inputs(seed: int = 0) -> dict:
    splits = jax.random.split(jax.random.key(seed), 5)
    queries = draw_queries(jax.random.fold_in(splits[4], 71), 0)
    keys = draw_keys(jax.random.fold_in(splits[4], 71), 0)
    values = gaussian(splits[2], (TOKENS, KVH * HD), 1.0, 6.0, ((0, 512),))
    segments = jnp.searchsorted(jnp.cumsum(ragged_sizes(splits[3], DOCS, TOKENS, MOST_DOC, 2)), jnp.arange(TOKENS), side="right").astype(jnp.int32)
    return {"queries": queries, "keys": keys, "values": values, "segments": segments}


def attend(q_blk, k_blk, v_blk, q_start, k_start, q_seg, k_seg):
    rows = q_blk.shape[0]
    kv_count = k_blk.shape[1] // HD
    group = (q_blk.shape[1] // HD) // kv_count
    q_pos = q_start + jnp.arange(rows, dtype=jnp.int32)
    k_pos = k_start + jnp.arange(rows, dtype=jnp.int32)
    allowed = (k_pos[None, :] <= q_pos[:, None]) & (q_pos[:, None] - k_pos[None, :] < 2 * rows) & (q_seg[:, None] == k_seg[None, :])
    outs, tops, totals = [], [], []
    for head_kv in range(kv_count):
        q_head = q_blk[:, head_kv * group * HD:(head_kv + 1) * group * HD].reshape(rows, group, HD).astype(jnp.float32)
        k_head = k_blk[:, head_kv * HD:(head_kv + 1) * HD].astype(jnp.float32)
        v_head = v_blk[:, head_kv * HD:(head_kv + 1) * HD].astype(jnp.float32)
        scores = jnp.einsum("qrd,kd->rqk", q_head, k_head) * (HD ** -0.5)
        top = jnp.max(jnp.where(allowed, scores, -1e30), axis=-1)
        prob = jnp.where(allowed, jnp.exp(scores - top[..., None]), 0.0)
        totals.append(jnp.sum(prob, axis=-1))
        tops.append(top)
        rounded = lax.optimization_barrier(prob.astype(jnp.bfloat16)).astype(jnp.float32)
        outs.append(jnp.einsum("rqk,kd->qrd", rounded, v_head).reshape(rows, group * HD))
    return jnp.concatenate(outs, axis=1), jnp.concatenate(tops, axis=0), jnp.concatenate(totals, axis=0)


def combine(parts):
    highest = parts[0][1]
    for part in parts[1:]:
        highest = jnp.maximum(highest, part[1])
    numer = 0.0
    denom = 0.0
    for outp, top, total in parts:
        weight = jnp.exp(top - highest)
        numer = numer + outp * jnp.repeat(weight.T, HD, axis=1)
        denom = denom + jnp.repeat((weight * total).T, HD, axis=1)
    return (numer / denom).astype(jnp.bfloat16)


def reference(queries, keys, values, segments):
    rows = BLOCK
    count = TOKENS // BLOCK
    zeros = jnp.zeros((2 * rows, KVH * HD), keys.dtype)
    key_pad = jnp.concatenate([zeros, keys], axis=0)
    value_pad = jnp.concatenate([zeros, values], axis=0)
    seg_pad = jnp.concatenate([jnp.full((2 * rows,), -1, jnp.int32), segments.astype(jnp.int32)])

    def one_block(index):
        q_blk = lax.dynamic_slice_in_dim(queries, (index * rows).astype(jnp.int32), rows)
        q_seg = lax.dynamic_slice_in_dim(seg_pad, ((index + 2) * rows).astype(jnp.int32), rows)
        parts = []
        for dist in range(3):
            start = ((index - dist + 2) * rows).astype(jnp.int32)
            k_blk = lax.dynamic_slice_in_dim(key_pad, start, rows)
            v_blk = lax.dynamic_slice_in_dim(value_pad, start, rows)
            k_seg = lax.dynamic_slice_in_dim(seg_pad, start, rows)
            parts.append(attend(q_blk, k_blk, v_blk, index * rows, (index - dist) * rows, q_seg, k_seg))
        return combine(parts)

    blocks = lax.map(one_block, jnp.arange(count, dtype=jnp.int32))
    return blocks.reshape(TOKENS, H * HD)
```

```python
import math
import jax
import jax.numpy as jnp
from jax import lax
from jax.experimental import pallas as pl
from jax.experimental.pallas import tpu as pltpu
from jax.sharding import PartitionSpec as P

HD = 128
HALF = 128
WINDOW = 512
BOTH = ("ctx", "head")
EXP2_SCALE = HD ** (-0.5) * math.log2(math.e)


def attention_kernel(seg_ref, q_ref, a0, b0, a1, b1, a2, b2, out_ref, bias_ref):
    c = lax.axis_index("ctx")
    first = lax.axis_index("head") == 0
    kv_heads = a0.shape[1] // (2 * HD)
    group = q_ref.shape[1] // HD // kv_heads
    halves = 6
    seen = halves - 1

    row = lax.broadcasted_iota(jnp.int32, (HALF, HALF), 0)
    col = lax.broadcasted_iota(jnp.int32, (HALF, HALF), 1)
    for qb in range(2):
        q_seg = jnp.broadcast_to(seg_ref[pl.ds(2 * c + qb, 1), :], (HALF, HALF)).T
        for t in range(seen):
            key_half = 2 * c - 4 + qb + t
            k_seg = seg_ref[pl.ds(jnp.maximum(key_half, 0), 1), :]
            ok = (q_seg == k_seg) & (key_half >= 0)
            if t == seen - 1:
                ok = ok & (col <= row)
            if t == 0:
                ok = ok & (col > row)
            bias_ref[qb, :, t * HALF : (t + 1) * HALF] = jnp.where(ok, 0.0, -jnp.inf)

    ones = jnp.ones((halves * HALF, HD), jnp.bfloat16)
    for g in range(kv_heads):
        def both_halves(near, cross, at):
            x = near[:, at * HD : (at + 1) * HD]
            y = cross[:, at * HD : (at + 1) * HD]
            return [jnp.where(first, x, y), jnp.where(first, y, x)]

        k_all, v_all = [], []
        for near, cross in ((a2, b2), (a1, b1), (a0, b0)):
            k_all += both_halves(near, cross, g)
            v_all += both_halves(near, cross, kv_heads + g)
        k_all = jnp.concatenate(k_all, axis=0)
        v_all = jnp.concatenate([jnp.concatenate(v_all, axis=0), ones], axis=1)
        for qb in range(2):
            rows = slice(qb * HALF, (qb + 1) * HALF)
            q = jnp.concatenate(
                [q_ref[rows, (g * group + r) * HD : (g * group + r + 1) * HD] for r in range(group)], axis=0
            )
            k = k_all[qb * HALF : (qb + seen) * HALF]
            v = v_all[qb * HALF : (qb + seen) * HALF]
            s = lax.dot_general(q, k, (((1,), (1,)), ((), ())), preferred_element_type=jnp.float32)
            s = s.reshape(group, HALF, seen * HALF) + bias_ref[qb][None]
            top = jnp.max(s, axis=-1, keepdims=True)
            p = jnp.exp2((s - top) * EXP2_SCALE).astype(jnp.bfloat16)
            o = jnp.dot(p.reshape(group * HALF, seen * HALF), v, preferred_element_type=jnp.float32)
            o = (o[:, :HD] / o[:, HD:]).astype(jnp.bfloat16)
            for r in range(group):
                out_ref[rows, (g * group + r) * HD : (g * group + r + 1) * HD] = o[r * HALF : (r + 1) * HALF]


def attention(seg, q, *pieces):
    vmem = pl.BlockSpec(memory_space=pltpu.VMEM)
    return pl.pallas_call(
        attention_kernel,
        out_shape=jax.ShapeDtypeStruct(q.shape, q.dtype),
        in_specs=[vmem] * (2 + len(pieces)),
        out_specs=vmem,
        scratch_shapes=[pltpu.VMEM((2, HALF, 5 * HALF), jnp.float32)],
        compiler_params=pltpu.CompilerParams(vmem_limit_bytes=40 * 1024 * 1024),
    )(seg, q, *pieces)


def send(x, by, cross):
    blocks = lax.axis_size("ctx")
    pairs = [
        (2 * i + h, 2 * (i + by) + (1 - h if cross else h)) for i in range(blocks - by) for h in range(2)
    ]
    return lax.ppermute(x, BOTH, pairs)


def body(queries, keys, values, segments):
    h = lax.axis_index("head")
    width = keys.shape[1] // 2

    def columns(x, which):
        return lax.dynamic_slice_in_dim(x, which * width, width, axis=1)

    near = jnp.concatenate([columns(keys, h), columns(values, h)], axis=1)
    cross = jnp.concatenate([columns(keys, 1 - h), columns(values, 1 - h)], axis=1)
    a2 = send(near, 2, False)
    b2 = send(cross, 2, True)
    a1 = send(near, 1, False)
    b1 = send(cross, 1, True)
    b0 = send(cross, 0, True)
    return attention(segments.reshape(-1, HALF), queries, near, b0, a1, b1, a2, b2)


def solution(mesh):
    placed = (P("ctx", "head"), P(("ctx", "head"), None), P(("ctx", "head"), None), P())
    return jax.shard_map(
        body, mesh=mesh, in_specs=placed, out_specs=P("ctx", "head"), check_vma=False
    )
```

```python
import math
import jax
import jax.numpy as jnp
from jax import lax
from jax.experimental import pallas as pl
from jax.experimental.pallas import tpu as pltpu
from jax.sharding import PartitionSpec as P

HD = 128
HALF = 128
BLOCK = 2 * HALF
KV = 4
BOTH = ("ctx", "head")
EXP2_SCALE = HD ** (-0.5) * math.log2(math.e)
VMEM = pl.BlockSpec(memory_space=pltpu.VMEM)
STATE = (jax.ShapeDtypeStruct((2 * KV, 4 * HALF, HD), jnp.float32),) * 3
BIAS = jax.ShapeDtypeStruct((2, HALF, 6 * HALF), jnp.float32)


def is_first():
    return lax.axis_index("head") == 0


def is_even():
    return lax.rem(lax.axis_index("ctx"), 2) == 0


def put_masks(seg_ref, bias_ref):
    c = lax.axis_index("ctx")
    row = lax.broadcasted_iota(jnp.int32, (HALF, HALF), 0)
    col = lax.broadcasted_iota(jnp.int32, (HALF, HALF), 1)
    for qb in range(2):
        q_seg = jnp.broadcast_to(seg_ref[pl.ds(2 * c + qb, 1), :], (HALF, HALF)).T
        for t in range(6):
            key_half = 2 * c - 4 + t
            k_seg = seg_ref[pl.ds(jnp.maximum(key_half, 0), 1), :]
            ok = (q_seg == k_seg) & (key_half >= 0)
            if t == qb + 4:
                ok = ok & (col <= row)
            if t == qb:
                ok = ok & (col > row)
            if t - qb not in range(5):
                ok = jnp.zeros_like(ok)
            bias_ref[qb, :, t * HALF : (t + 1) * HALF] = jnp.where(ok, 0.0, -jnp.inf)


def fold(q_ref, g, qb, k, v, bias, old, new):
    group = q_ref.shape[1] // (KV * HD)
    at, count = KV * qb + g, k.shape[0]
    q = jnp.concatenate(
        [
            q_ref[qb * HALF : (qb + 1) * HALF, (g * group + r) * HD : (g * group + r + 1) * HD]
            for r in range(group)
        ],
        axis=0,
    )
    s = lax.dot_general(q, k, (((1,), (1,)), ((), ())), preferred_element_type=jnp.float32)
    s = (s.reshape(group, HALF, count) + bias[None]).reshape(group * HALF, count)
    before = jnp.full((group * HALF, HD), -1e30, jnp.float32) if old is None else old[0][at]
    top = jnp.maximum(before, jnp.max(s, axis=-1, keepdims=True))
    p = jnp.exp2((s - jnp.concatenate([top] * (count // HD), axis=1)) * EXP2_SCALE).astype(jnp.bfloat16)
    v = jnp.concatenate([v, jnp.ones_like(v)], axis=1)
    o = jnp.dot(p, v, preferred_element_type=jnp.float32)
    acc, total = o[:, :HD], o[:, HD:]
    if old is not None:
        keep = jnp.exp2((before - top) * EXP2_SCALE)
        acc = acc + old[1][at] * keep
        total = total + old[2][at] * keep
    if new is not None:
        new[0][at], new[1][at], new[2][at] = top, acc, total
    return acc, total


def head_of(ref, at):
    return ref[:, at * HD : (at + 1) * HD]


def halves(first, near, cross):
    return [jnp.where(first, near, cross), jnp.where(first, cross, near)]


def half_bias(bias_ref, qb, t):
    return bias_ref[qb, :, t * HALF : (t + 1) * HALF]


def near_kernel(seg_ref, q_ref, x1, x2, bias_ref, *new):
    put_masks(seg_ref, bias_ref)
    first, even = is_first(), is_even()
    for g in range(KV):
        k, v = (jnp.where(even, head_of(x2, at), head_of(x1, at)) for at in (g, KV + g))
        for qb in range(2):
            bias = jnp.where(first, half_bias(bias_ref, qb, 4), half_bias(bias_ref, qb, 5))
            fold(q_ref, g, qb, k, v, bias, None, new)


def cross_bias(first, bias_ref, qb):
    return jnp.where(first, half_bias(bias_ref, qb, 5), half_bias(bias_ref, qb, 4))


def even_own_kernel(q_ref, bias_ref, x2, r1, *new):
    first = is_first()

    @pl.when(is_even())
    def _():
        for g in range(KV):
            k, v = (jnp.concatenate(halves(first, head_of(x2, at), head_of(r1, at)), axis=0) for at in (g, KV + g))
            for qb in range(2):
                seen = HALF * (qb + 1)
                fold(q_ref, g, qb, k[:seen], v[:seen], bias_ref[qb, :, 2 * BLOCK : 2 * BLOCK + seen], None, new)


def previous_kernel(q_ref, bias_ref, near_pair, cross_pair, *state):
    first, even = is_first(), is_even()
    new = state[6:]

    def step(at_core, old):
        for g in range(KV):
            k, v = (
                jnp.concatenate(halves(first, *(head_of(x, at)[at_core] for x in (near_pair, cross_pair))), axis=0)
                for at in (g, KV + g)
            )
            for qb in range(2):
                fold(q_ref, g, qb, k, v, bias_ref[qb, :, BLOCK : 2 * BLOCK], old, new)

    @pl.when(even)
    def _():
        step(slice(HALF, BLOCK), state[3:6])

    @pl.when(jnp.logical_not(even))
    def _():
        step(slice(0, HALF), state[:3])


def last_kernel(q_ref, bias_ref, r1, r2, r3, r4, *rest):
    old, (out_ref, rows_ref, sems) = rest[:3], rest[3:]
    first, even = is_first(), is_even()
    group = q_ref.shape[1] // (KV * HD)

    def finish(near, cross, own):
        copies = []
        for g in range(KV):
            kv = []
            for at in (g, KV + g):
                parts = halves(first, head_of(near, at), head_of(cross, at))
                kv.append(jnp.concatenate(parts if own is None else parts + [head_of(own, at)], axis=0))
            for qb in range(2):
                k, v = (x[qb * HALF :] for x in kv)
                bias = bias_ref[qb, :, qb * HALF : BLOCK]
                if own is not None:
                    bias = jnp.concatenate([bias, cross_bias(first, bias_ref, qb)], axis=1)
                acc, total = fold(q_ref, g, qb, k, v, bias, old, None)
                guess = pl.reciprocal(total, approx=True)
                res = (acc * (guess * (2.0 - total * guess))).astype(jnp.bfloat16)
                for r in range(group):
                    cols = slice((g * group + r) * HD, (g * group + r + 1) * HD)
                    rows_ref[qb * HALF : (qb + 1) * HALF, cols] = res[r * HALF : (r + 1) * HALF]
            cols = pl.ds(g * group * HD, group * HD)
            copies.append(pltpu.make_async_copy(rows_ref.at[:, cols], out_ref.at[:, cols], sems.at[g]))
            copies[-1].start()
        for copy in copies:
            copy.wait()

    @pl.when(even)
    def _():
        finish(r3, r4, None)

    @pl.when(jnp.logical_not(even))
    def _():
        finish(r1, r2, r3)


def call(kernel, outs, *args, out_specs=None, scratch=()):
    return pl.pallas_call(
        kernel,
        out_shape=outs,
        in_specs=[VMEM] * len(args),
        out_specs=jax.tree.map(lambda _: VMEM, outs) if out_specs is None else out_specs,
        scratch_shapes=scratch,
        compiler_params=pltpu.CompilerParams(vmem_limit_bytes=24 * 1024 * 1024),
    )(*args)


def call_last(queries, *args):
    return call(
        last_kernel,
        jax.ShapeDtypeStruct(queries.shape, queries.dtype),
        queries,
        *args,
        out_specs=pl.BlockSpec(memory_space=pl.ANY),
        scratch=[pltpu.VMEM(queries.shape, queries.dtype), pltpu.SemaphoreType.DMA((KV,))],
    )


def send(x, odd, even):
    blocks = lax.axis_size("ctx")
    pairs = []
    for i in range(blocks):
        move = odd if i % 2 else even
        if move is not None and i + move[0] < blocks:
            pairs += [(2 * i + h, 2 * (i + move[0]) + (1 - h if move[1] else h)) for h in range(2)]
    return lax.ppermute(x, BOTH, pairs)


def core_pair(x):
    blocks = lax.axis_size("ctx")
    return lax.all_gather(x, "ctx", axis=0, tiled=True, axis_index_groups=[[i, i + 1] for i in range(0, blocks, 2)])


def body(queries, keys, values, segments):
    h = lax.axis_index("head")
    width = keys.shape[1] // 2

    def columns(x, which):
        return lax.dynamic_slice_in_dim(x, which * width, width, axis=1)

    even = is_even()
    which = jnp.where(even, 1 - h, h)
    x1 = jnp.concatenate([columns(keys, which), columns(values, which)], axis=1)
    x2 = jnp.concatenate([columns(keys, 1 - which), columns(values, 1 - which)], axis=1)
    r1 = send(x1, odd=(2, False), even=(0, True))
    r2 = send(x2, odd=(2, True), even=None)
    bias, *state = call(near_kernel, (BIAS,) + STATE, segments.reshape(-1, HALF), queries, x1, x2)
    x1_later, x2_later, bias = lax.optimization_barrier((x1, x2, bias))
    r3 = send(x2_later, odd=(0, True), even=(2, False))
    r4 = send(x1_later, odd=None, even=(2, True))
    even_state = call(even_own_kernel, STATE, queries, bias, x2, r1)
    r1_later, *even_state = lax.optimization_barrier((r1, *even_state))
    near_pair = core_pair(jnp.where(even, x2, r1_later))
    r2_later, near_pair = lax.optimization_barrier((r2, near_pair))
    cross_pair = core_pair(jnp.where(even, r1, r2_later))
    state = call(previous_kernel, STATE, queries, bias, near_pair, cross_pair, *state, *even_state)
    return call_last(queries, bias, r1, r2, r3, r4, *state)


def solution(mesh):
    placed = (P("ctx", "head"), P(("ctx", "head"), None), P(("ctx", "head"), None), P())
    return jax.shard_map(
        body, mesh=mesh, in_specs=placed, out_specs=P("ctx", "head"), check_vma=False
    )
```

```python
import functools
import math
import jax
import jax.numpy as jnp
from jax import lax
from jax.experimental import pallas as pl
from jax.experimental.pallas import tpu as pltpu
from jax.sharding import PartitionSpec as P

HD = 128
HALF = 128
BLOCK = 2 * HALF
KV = 4
FAR = 64.0
BOTH = ("ctx", "head")
EXP2_SCALE = HD ** (-0.5) * math.log2(math.e)
VMEM = pl.BlockSpec(memory_space=pltpu.VMEM)
STATE = (jax.ShapeDtypeStruct((2 * KV, 4 * HALF, HD), jnp.float32),) * 3
BIAS = jax.ShapeDtypeStruct((2, HALF, 6 * HALF), jnp.float32)


def is_first():
    return lax.axis_index("head") == 0


def is_even():
    return lax.rem(lax.axis_index("ctx"), 2) == 0


def put_masks(seg_ref, bias_ref):
    c = lax.axis_index("ctx")
    row = lax.broadcasted_iota(jnp.int32, (HALF, HALF), 0)
    col = lax.broadcasted_iota(jnp.int32, (HALF, HALF), 1)
    for qb in range(2):
        q_seg = jnp.broadcast_to(seg_ref[pl.ds(2 * c + qb, 1), :], (HALF, HALF)).T
        for t in range(6):
            key_half = 2 * c - 4 + t
            k_seg = seg_ref[pl.ds(jnp.maximum(key_half, 0), 1), :]
            ok = (q_seg == k_seg) & (key_half >= 0)
            if t == qb + 4:
                ok = ok & (col <= row)
            if t == qb:
                ok = ok & (col > row)
            if t - qb not in range(5):
                ok = jnp.zeros_like(ok)
            bias_ref[qb, :, t * HALF : (t + 1) * HALF] = jnp.where(ok, 0.0, -jnp.inf)


def fold(q_ref, g, qb, k, v, bias, old, new):
    group = q_ref.shape[1] // (KV * HD)
    at, count = KV * qb + g, k.shape[0]
    q = jnp.concatenate(
        [
            q_ref[qb * HALF : (qb + 1) * HALF, (g * group + r) * HD : (g * group + r + 1) * HD]
            for r in range(group)
        ],
        axis=0,
    )
    s = lax.dot_general(q, k, (((1,), (1,)), ((), ())), preferred_element_type=jnp.float32)
    s = (s.reshape(group, HALF, count) + bias[None]).reshape(group * HALF, count)
    before = jnp.full((group * HALF, HD), -1e30, jnp.float32) if old is None else old[0][at]
    top = jnp.maximum(before, jnp.max(s, axis=-1, keepdims=True))
    p = jnp.exp2((s - jnp.concatenate([top] * (count // HD), axis=1)) * EXP2_SCALE).astype(jnp.bfloat16)
    v = jnp.concatenate([v, jnp.ones_like(v)], axis=1)
    o = jnp.dot(p, v, preferred_element_type=jnp.float32)
    acc, total = o[:, :HD], o[:, HD:]
    if old is not None:
        keep = jnp.exp2((before - top) * EXP2_SCALE)
        acc = acc + old[1][at] * keep
        total = total + old[2][at] * keep
    if new is not None:
        new[0][at], new[1][at], new[2][at] = top, acc, total
    return acc, total


def fold_unmoved(q_ref, g, qb, k, v, bias, old):
    group = q_ref.shape[1] // (KV * HD)
    at, count = KV * qb + g, k.shape[0]
    q = jnp.concatenate(
        [
            q_ref[qb * HALF : (qb + 1) * HALF, (g * group + r) * HD : (g * group + r + 1) * HD]
            for r in range(group)
        ],
        axis=0,
    )
    s = lax.dot_general(q, k, (((1,), (1,)), ((), ())), preferred_element_type=jnp.float32)
    s = (s.reshape(group, HALF, count) + bias[None]).reshape(group * HALF, count)
    above = (s - jnp.concatenate([old[0][at]] * (count // HD), axis=1)) * EXP2_SCALE
    v = jnp.concatenate([v, jnp.ones_like(v)], axis=1)
    o = jnp.dot(jnp.exp2(above).astype(jnp.bfloat16), v, preferred_element_type=jnp.float32)
    highest = functools.reduce(jnp.maximum, [above[:, n * HD : (n + 1) * HD] for n in range(count // HD)])
    highest = jnp.max(highest.reshape(-1, 8, HD), axis=0)
    return o[:, :HD] + old[1][at], o[:, HD:] + old[2][at], highest


def head_of(ref, at):
    return ref[:, at * HD : (at + 1) * HD]


def halves(first, near, cross):
    return [jnp.where(first, near, cross), jnp.where(first, cross, near)]


def half_bias(bias_ref, qb, t):
    return bias_ref[qb, :, t * HALF : (t + 1) * HALF]


def near_kernel(seg_ref, q_ref, x1, x2, bias_ref, *new):
    put_masks(seg_ref, bias_ref)
    first, even = is_first(), is_even()
    for g in range(KV):
        k, v = (jnp.where(even, head_of(x2, at), head_of(x1, at)) for at in (g, KV + g))
        for qb in range(2):
            bias = jnp.where(first, half_bias(bias_ref, qb, 4), half_bias(bias_ref, qb, 5))
            fold(q_ref, g, qb, k, v, bias, None, new)


def cross_bias(first, bias_ref, qb):
    return jnp.where(first, half_bias(bias_ref, qb, 5), half_bias(bias_ref, qb, 4))


def even_own_kernel(q_ref, bias_ref, x2, r1, *new):
    first = is_first()

    @pl.when(is_even())
    def _():
        for g in range(KV):
            k, v = (jnp.concatenate(halves(first, head_of(x2, at), head_of(r1, at)), axis=0) for at in (g, KV + g))
            for qb in range(2):
                seen = HALF * (qb + 1)
                fold(q_ref, g, qb, k[:seen], v[:seen], bias_ref[qb, :, 2 * BLOCK : 2 * BLOCK + seen], None, new)


def previous_kernel(q_ref, bias_ref, near_pair, cross_pair, *state):
    first, even = is_first(), is_even()
    new = state[6:]

    def step(at_core, old):
        for g in range(KV):
            k, v = (
                jnp.concatenate(halves(first, *(head_of(x, at)[at_core] for x in (near_pair, cross_pair))), axis=0)
                for at in (g, KV + g)
            )
            for qb in range(2):
                fold(q_ref, g, qb, k, v, bias_ref[qb, :, BLOCK : 2 * BLOCK], old, new)

    @pl.when(even)
    def _():
        step(slice(HALF, BLOCK), state[3:6])

    @pl.when(jnp.logical_not(even))
    def _():
        step(slice(0, HALF), state[:3])


def last_kernel(q_ref, bias_ref, r1, r2, r3, r4, *rest):
    old, (out_ref, rows_ref, sems) = rest[:3], rest[3:]
    first, even = is_first(), is_even()
    group = q_ref.shape[1] // (KV * HD)

    def finish(near, cross, own, unmoved):
        copies, highest = [], None
        for g in range(KV):
            kv = []
            for at in (g, KV + g):
                parts = halves(first, head_of(near, at), head_of(cross, at))
                kv.append(jnp.concatenate(parts if own is None else parts + [head_of(own, at)], axis=0))
            for qb in range(2):
                k, v = (x[qb * HALF :] for x in kv)
                bias = bias_ref[qb, :, qb * HALF : BLOCK]
                if own is not None:
                    bias = jnp.concatenate([bias, cross_bias(first, bias_ref, qb)], axis=1)
                if unmoved:
                    acc, total, high = fold_unmoved(q_ref, g, qb, k, v, bias, old)
                    highest = high if highest is None else jnp.maximum(highest, high)
                else:
                    acc, total = fold(q_ref, g, qb, k, v, bias, old, None)
                res = (acc * pltpu.reciprocal(total, approx=True)).astype(jnp.bfloat16)
                for r in range(group):
                    cols = slice((g * group + r) * HD, (g * group + r + 1) * HD)
                    rows_ref[qb * HALF : (qb + 1) * HALF, cols] = res[r * HALF : (r + 1) * HALF]
            cols = pl.ds(g * group * HD, group * HD)
            copies.append(pltpu.make_async_copy(rows_ref.at[:, cols], out_ref.at[:, cols], sems.at[g]))
            copies[-1].start()
        far = jnp.logical_not(jnp.max(highest) <= FAR) if unmoved else None
        for copy in copies:
            copy.wait()
        return far

    @pl.when(even)
    def _():
        far = finish(r3, r4, None, True)

        @pl.when(far)
        def _():
            finish(r3, r4, None, False)

    @pl.when(jnp.logical_not(even))
    def _():
        finish(r1, r2, r3, False)


def call(kernel, outs, *args, out_specs=None, scratch=()):
    return pl.pallas_call(
        kernel,
        out_shape=outs,
        in_specs=[VMEM] * len(args),
        out_specs=jax.tree.map(lambda _: VMEM, outs) if out_specs is None else out_specs,
        scratch_shapes=scratch,
        compiler_params=pltpu.CompilerParams(vmem_limit_bytes=24 * 1024 * 1024),
    )(*args)


def call_last(queries, *args):
    return call(
        last_kernel,
        jax.ShapeDtypeStruct(queries.shape, queries.dtype),
        queries,
        *args,
        out_specs=pl.BlockSpec(memory_space=pl.ANY),
        scratch=[pltpu.VMEM(queries.shape, queries.dtype), pltpu.SemaphoreType.DMA((KV,))],
    )


def send(x, odd, even):
    blocks = lax.axis_size("ctx")
    pairs = []
    for i in range(blocks):
        move = odd if i % 2 else even
        if move is not None and i + move[0] < blocks:
            pairs += [(2 * i + h, 2 * (i + move[0]) + (1 - h if move[1] else h)) for h in range(2)]
    return lax.ppermute(x, BOTH, pairs)


def core_pair(x):
    blocks = lax.axis_size("ctx")
    return lax.all_gather(x, "ctx", axis=0, tiled=True, axis_index_groups=[[i, i + 1] for i in range(0, blocks, 2)])


def body(queries, keys, values, segments):
    h = lax.axis_index("head")
    width = keys.shape[1] // 2

    def columns(x, which):
        return lax.dynamic_slice_in_dim(x, which * width, width, axis=1)

    even = is_even()
    which = jnp.where(even, 1 - h, h)
    x1 = jnp.concatenate([columns(keys, which), columns(values, which)], axis=1)
    x2 = jnp.concatenate([columns(keys, 1 - which), columns(values, 1 - which)], axis=1)
    r1 = send(x1, odd=(2, False), even=(0, True))
    r2 = send(x2, odd=(2, True), even=None)
    bias, *state = call(near_kernel, (BIAS,) + STATE, segments.reshape(-1, HALF), queries, x1, x2)
    x1_later, x2_later, bias = lax.optimization_barrier((x1, x2, bias))
    r3 = send(x2_later, odd=(0, True), even=(2, False))
    r4 = send(x1_later, odd=None, even=(2, True))
    even_state = call(even_own_kernel, STATE, queries, bias, x2, r1)
    r1_later, *even_state = lax.optimization_barrier((r1, *even_state))
    near_pair = core_pair(jnp.where(even, x2, r1_later))
    r2_later, near_pair = lax.optimization_barrier((r2, near_pair))
    cross_pair = core_pair(jnp.where(even, r1, r2_later))
    state = call(previous_kernel, STATE, queries, bias, near_pair, cross_pair, *state, *even_state)
    return call_last(queries, bias, r1, r2, r3, r4, *state)


def solution(mesh):
    placed = (P("ctx", "head"), P(("ctx", "head"), None), P(("ctx", "head"), None), P())
    return jax.shard_map(
        body, mesh=mesh, in_specs=placed, out_specs=P("ctx", "head"), check_vma=False
    )
```

```python
import functools
import math
import jax
import jax.numpy as jnp
from jax import lax
from jax.experimental import pallas as pl
from jax.experimental.pallas import tpu as pltpu
from jax.sharding import PartitionSpec as P

HD = 128
HALF = 128
BLOCK = 2 * HALF
KV = 4
FAR = 64.0
BOTH = ("ctx", "head")
EXP2_SCALE = HD ** (-0.5) * math.log2(math.e)
VMEM = pl.BlockSpec(memory_space=pltpu.VMEM)
STATE = (jax.ShapeDtypeStruct((2 * KV, 4 * HALF, HD), jnp.float32),) * 3
BIAS = jax.ShapeDtypeStruct((2, HALF, 6 * HALF), jnp.float32)


def is_first():
    return lax.axis_index("head") == 0


def is_even():
    return lax.rem(lax.axis_index("ctx"), 2) == 0


def put_masks(seg_ref, bias_ref):
    c = lax.axis_index("ctx")
    row = lax.broadcasted_iota(jnp.int32, (HALF, HALF), 0)
    col = lax.broadcasted_iota(jnp.int32, (HALF, HALF), 1)
    for qb in range(2):
        q_seg = jnp.broadcast_to(seg_ref[pl.ds(2 * c + qb, 1), :], (HALF, HALF)).T
        for t in range(6):
            key_half = 2 * c - 4 + t
            k_seg = seg_ref[pl.ds(jnp.maximum(key_half, 0), 1), :]
            ok = (q_seg == k_seg) & (key_half >= 0)
            if t == qb + 4:
                ok = ok & (col <= row)
            if t == qb:
                ok = ok & (col > row)
            if t - qb not in range(5):
                ok = jnp.zeros_like(ok)
            bias_ref[qb, :, t * HALF : (t + 1) * HALF] = jnp.where(ok, 0.0, -jnp.inf)


def fold(q_ref, g, qb, k, v, bias, old, new):
    group = q_ref.shape[1] // (KV * HD)
    at, count = KV * qb + g, k.shape[0]
    q = jnp.concatenate(
        [
            q_ref[qb * HALF : (qb + 1) * HALF, (g * group + r) * HD : (g * group + r + 1) * HD]
            for r in range(group)
        ],
        axis=0,
    )
    s = lax.dot_general(q, k, (((1,), (1,)), ((), ())), preferred_element_type=jnp.float32)
    s = (s.reshape(group, HALF, count) + bias[None]).reshape(group * HALF, count)
    before = jnp.full((group * HALF, HD), -1e30, jnp.float32) if old is None else old[0][at]
    top = jnp.maximum(before, jnp.max(s, axis=-1, keepdims=True))
    p = jnp.exp2((s - jnp.concatenate([top] * (count // HD), axis=1)) * EXP2_SCALE).astype(jnp.bfloat16)
    v = jnp.concatenate([v, jnp.ones_like(v)], axis=1)
    o = jnp.dot(p, v, preferred_element_type=jnp.float32)
    acc, total = o[:, :HD], o[:, HD:]
    if old is not None:
        keep = jnp.exp2((before - top) * EXP2_SCALE)
        acc = acc + old[1][at] * keep
        total = total + old[2][at] * keep
    if new is not None:
        new[0][at], new[1][at], new[2][at] = top, acc, total
    return acc, total


def fold_unmoved(q_ref, g, qb, k, v, bias, old):
    group = q_ref.shape[1] // (KV * HD)
    at, count = KV * qb + g, k.shape[0]
    q = jnp.concatenate(
        [
            q_ref[qb * HALF : (qb + 1) * HALF, (g * group + r) * HD : (g * group + r + 1) * HD]
            for r in range(group)
        ],
        axis=0,
    )
    s = lax.dot_general(q, k, (((1,), (1,)), ((), ())), preferred_element_type=jnp.float32)
    s = (s.reshape(group, HALF, count) + bias[None]).reshape(group * HALF, count)
    above = (s - jnp.concatenate([old[0][at]] * (count // HD), axis=1)) * EXP2_SCALE
    v = jnp.concatenate([v, jnp.ones_like(v)], axis=1)
    o = jnp.dot(jnp.exp2(above).astype(jnp.bfloat16), v, preferred_element_type=jnp.float32)
    highest = functools.reduce(jnp.maximum, [above[:, n * HD : (n + 1) * HD] for n in range(count // HD)])
    highest = jnp.max(highest.reshape(-1, 8, HD), axis=0)
    return o[:, :HD] + old[1][at], o[:, HD:] + old[2][at], highest


def head_of(ref, at):
    return ref[:, at * HD : (at + 1) * HD]


def halves(first, near, cross):
    return [jnp.where(first, near, cross), jnp.where(first, cross, near)]


def half_bias(bias_ref, qb, t):
    return bias_ref[qb, :, t * HALF : (t + 1) * HALF]


def near_kernel(seg_ref, q_ref, x1, x2, bias_ref, *new):
    put_masks(seg_ref, bias_ref)
    first, even = is_first(), is_even()
    for g in range(KV):
        k, v = (jnp.where(even, head_of(x2, at), head_of(x1, at)) for at in (g, KV + g))
        for qb in range(2):
            bias = jnp.where(first, half_bias(bias_ref, qb, 4), half_bias(bias_ref, qb, 5))
            fold(q_ref, g, qb, k, v, bias, None, new)


def cross_bias(first, bias_ref, qb):
    return jnp.where(first, half_bias(bias_ref, qb, 5), half_bias(bias_ref, qb, 4))


def even_own_kernel(q_ref, bias_ref, x2, r1, *new):
    first = is_first()

    @pl.when(is_even())
    def _():
        for g in range(KV):
            k, v = (jnp.concatenate(halves(first, head_of(x2, at), head_of(r1, at)), axis=0) for at in (g, KV + g))
            for qb in range(2):
                seen = HALF * (qb + 1)
                fold(q_ref, g, qb, k[:seen], v[:seen], bias_ref[qb, :, 2 * BLOCK : 2 * BLOCK + seen], None, new)


def previous_kernel(q_ref, bias_ref, near_pair, cross_pair, *state):
    first, even = is_first(), is_even()
    new = state[6:]

    def step(at_core, old):
        for g in range(KV):
            k, v = (
                jnp.concatenate(halves(first, *(head_of(x, at)[at_core] for x in (near_pair, cross_pair))), axis=0)
                for at in (g, KV + g)
            )
            for qb in range(2):
                fold(q_ref, g, qb, k, v, bias_ref[qb, :, BLOCK : 2 * BLOCK], old, new)

    @pl.when(even)
    def _():
        step(slice(HALF, BLOCK), state[3:6])

    @pl.when(jnp.logical_not(even))
    def _():
        step(slice(0, HALF), state[:3])


def last_kernel(q_ref, bias_ref, r1, r2, r3, r4, *rest):
    old, (out_ref, rows_ref, sems) = rest[:3], rest[3:]
    first, even = is_first(), is_even()
    group = q_ref.shape[1] // (KV * HD)

    def finish(near, cross, own, unmoved):
        copies, highest = [], None
        for g in range(KV):
            kv = []
            for at in (g, KV + g):
                parts = halves(first, head_of(near, at), head_of(cross, at))
                kv.append(jnp.concatenate(parts if own is None else parts + [head_of(own, at)], axis=0))
            for qb in range(2):
                k, v = (x[qb * HALF :] for x in kv)
                bias = bias_ref[qb, :, qb * HALF : BLOCK]
                if own is not None:
                    bias = jnp.concatenate([bias, cross_bias(first, bias_ref, qb)], axis=1)
                if unmoved:
                    acc, total, high = fold_unmoved(q_ref, g, qb, k, v, bias, old)
                    highest = high if highest is None else jnp.maximum(highest, high)
                else:
                    acc, total = fold(q_ref, g, qb, k, v, bias, old, None)
                res = (acc * pltpu.reciprocal(total, approx=True)).astype(jnp.bfloat16)
                for r in range(group):
                    cols = slice((g * group + r) * HD, (g * group + r + 1) * HD)
                    rows_ref[qb * HALF : (qb + 1) * HALF, cols] = res[r * HALF : (r + 1) * HALF]
                if g == KV - 1 or qb == 1:
                    rows = slice(qb * HALF if g == KV - 1 else 0, (qb + 1) * HALF)
                    part = (rows, slice(g * group * HD, (g + 1) * group * HD))
                    copies.append(pltpu.make_async_copy(rows_ref.at[part], out_ref.at[part], sems.at[g + qb * (g == KV - 1)]))
                    copies[-1].start()
        far = jnp.logical_not(jnp.max(highest) <= FAR) if unmoved else None
        for copy in copies:
            copy.wait()
        return far

    @pl.when(even)
    def _():
        far = finish(r3, r4, None, True)

        @pl.when(far)
        def _():
            finish(r3, r4, None, False)

    @pl.when(jnp.logical_not(even))
    def _():
        finish(r1, r2, r3, False)


def call(kernel, outs, *args, out_specs=None, scratch=()):
    return pl.pallas_call(
        kernel,
        out_shape=outs,
        in_specs=[VMEM] * len(args),
        out_specs=jax.tree.map(lambda _: VMEM, outs) if out_specs is None else out_specs,
        scratch_shapes=scratch,
        compiler_params=pltpu.CompilerParams(vmem_limit_bytes=24 * 1024 * 1024),
    )(*args)


def call_last(queries, *args):
    return call(
        last_kernel,
        jax.ShapeDtypeStruct(queries.shape, queries.dtype),
        queries,
        *args,
        out_specs=pl.BlockSpec(memory_space=pl.ANY),
        scratch=[pltpu.VMEM(queries.shape, queries.dtype), pltpu.SemaphoreType.DMA((KV + 1,))],
    )


def send(x, odd, even):
    blocks = lax.axis_size("ctx")
    pairs = []
    for i in range(blocks):
        move = odd if i % 2 else even
        if move is not None and i + move[0] < blocks:
            pairs += [(2 * i + h, 2 * (i + move[0]) + (1 - h if move[1] else h)) for h in range(2)]
    return lax.ppermute(x, BOTH, pairs)


def core_pair(x):
    blocks = lax.axis_size("ctx")
    return lax.all_gather(x, "ctx", axis=0, tiled=True, axis_index_groups=[[i, i + 1] for i in range(0, blocks, 2)])


def body(queries, keys, values, segments):
    h = lax.axis_index("head")
    width = keys.shape[1] // 2

    def columns(x, which):
        return lax.dynamic_slice_in_dim(x, which * width, width, axis=1)

    even = is_even()
    which = jnp.where(even, 1 - h, h)
    x1 = jnp.concatenate([columns(keys, which), columns(values, which)], axis=1)
    x2 = jnp.concatenate([columns(keys, 1 - which), columns(values, 1 - which)], axis=1)
    r1 = send(x1, odd=(2, False), even=(0, True))
    r2 = send(x2, odd=(2, True), even=None)
    bias, *state = call(near_kernel, (BIAS,) + STATE, segments.reshape(-1, HALF), queries, x1, x2)
    x1_later, x2_later, bias = lax.optimization_barrier((x1, x2, bias))
    r3 = send(x2_later, odd=(0, True), even=(2, False))
    r4 = send(x1_later, odd=None, even=(2, True))
    even_state = call(even_own_kernel, STATE, queries, bias, x2, r1)
    r1_later, *even_state = lax.optimization_barrier((r1, *even_state))
    near_pair = core_pair(jnp.where(even, x2, r1_later))
    r2_later, near_pair = lax.optimization_barrier((r2, near_pair))
    cross_pair = core_pair(jnp.where(even, r1, r2_later))
    state = call(previous_kernel, STATE, queries, bias, near_pair, cross_pair, *state, *even_state)
    return call_last(queries, bias, r1, r2, r3, r4, *state)


def solution(mesh):
    placed = (P("ctx", "head"), P(("ctx", "head"), None), P(("ctx", "head"), None), P())
    return jax.shard_map(
        body, mesh=mesh, in_specs=placed, out_specs=P("ctx", "head"), check_vma=False
    )
```
